32 devices in a mesh: fsdp: 32 (over z, y, x, core).
Axes of the slice: x: 2, y: 2, z: 4, core: 2. Of those that a mesh axis runs over, the one named last changes fastest.
Arguments:
- tokens: bfloat16 [4096, 768], P('fsdp'), may hold values from -6 to 6
- lengths: int32 [64, 2], P('fsdp'), may hold values from 0 to 64, as said below
- cotangent: bfloat16 [4096, 768], P('fsdp'), may hold values from -6 to 6
- qkv_weight: bfloat16 [1769472], P('fsdp'), may hold values from -0.21875 to 0.21875
- out_weight: bfloat16 [589824], P('fsdp'), may hold values from -0.625 to 0.625
- up_weight: bfloat16 [2359296], P('fsdp'), may hold values from -0.21875 to 0.21875
- down_weight: bfloat16 [2359296], P('fsdp'), may hold values from -0.15625 to 0.15625
- norm_gains: bfloat16 [1536], P('fsdp'), may hold values from 0.5 to 1.5
- biases: bfloat16 [7680], P('fsdp'), may hold values from -1.796875 to 1.796875
Outputs:
- block_out: bfloat16 [4096, 768], P('fsdp')
- grad_tokens: bfloat16 [4096, 768], P('fsdp')
- grad_qkv: float32 [1769472], P('fsdp')
- grad_out_weight: float32 [589824], P('fsdp')
- grad_up: float32 [2359296], P('fsdp')
- grad_down: float32 [2359296], P('fsdp')
- grad_gains: float32 [1536], P('fsdp')
- grad_biases: float32 [7680], P('fsdp')
The draws below stay inside these ranges and needn't reach their ends.
Inputs may be any that keep to these rules, and one draw needn't show every extreme that they name: `lengths`: in each micro-batch of 64 rows the first sequence has 1 or more tokens and the two together fill 64 // 2 to 64 rows; the rows after them are padding. In every draw some micro-batch holds one sequence of 64 tokens.
All inputs are finite; a program needn't handle non-finite values.
Results may differ from the reference program's by a relative error of at most 0.01.
Values may be sent and summed in bfloat16 or wider, within the bound.
A program may use at most 192 MiB of HBM per device.

```python
import jax
import jax.numpy as jnp
from jax import lax

D = 768
H = 12
HD = 64
FF = 3072
ROWS = 64
BATCHES = 64
TOKENS = 4096


def draw_lengths(key, part):
    key = jax.random.fold_in(key, 7)
    key_total, key_first, key_full = jax.random.split(key, 3)
    live_total = jax.random.randint(key_total, (BATCHES,), ROWS // 2, ROWS + 1)
    full_slot = jax.random.randint(key_full, (), 0, BATCHES)
    slot_ids = jnp.arange(BATCHES, dtype=jnp.int32)
    live_total = jnp.where(slot_ids == full_slot, ROWS, live_total)
    first_len = jax.random.randint(key_first, (BATCHES,), 1, live_total + 1)
    first_len = jnp.where(slot_ids == full_slot, ROWS, first_len)
    return jnp.stack([first_len, live_total - first_len], axis=1).astype(jnp.int32)


def shard_levels(stream_key, dims, pieces, low, high):
    factor_of = 1.0
    for dim, blocks in pieces:
        draws = jax.random.uniform(jax.random.fold_in(jax.random.fold_in(stream_key, 6), dim), (blocks,), jnp.float32, low / len(pieces), high / len(pieces))
        factor_of = factor_of * jnp.repeat(jnp.exp(draws), dims[dim] // blocks).reshape((-1,) + (1,) * (len(dims) - 1 - dim))
    return factor_of


def normal_values(key, shape, scale, bound, cuts=(), held_as=jnp.bfloat16):
    factor_of = shard_levels(key, shape, cuts, -0.22, 0.18) if cuts else 1.0
    values = jax.random.normal(key, shape, jnp.float32) * scale * factor_of
    return jnp.minimum(jnp.maximum(values, -bound), bound).astype(held_as)


def setup_inputs(seed: int = 0) -> dict:
    streams_of = jax.random.split(jax.random.key(seed), 10)
    tokens = normal_values(streams_of[0], (TOKENS, D), 1.0, 6.0, ((0, 32),))
    lengths = draw_lengths(jax.random.fold_in(streams_of[9], 71), 0)
    cotangent = normal_values(streams_of[2], (TOKENS, D), 1.0, 6.0, ((0, 32),))
    qkv_weight = normal_values(streams_of[3], (3 * D * D,), D ** -0.5, 0.21875, ((0, 32),))
    out_weight = normal_values(streams_of[4], (D * D,), (D // 8) ** -0.5, 0.625, ((0, 32),))
    up_weight = normal_values(streams_of[5], (D * FF,), D ** -0.5, 0.21875, ((0, 32),))
    down_weight = normal_values(streams_of[6], (FF * D,), (FF // 2) ** -0.5, 0.15625, ((0, 32),))
    norm_gains = jnp.clip(1.0 + 0.1 * jax.random.normal(streams_of[7], (2 * D,), jnp.float32), 0.5, 1.5).astype(jnp.bfloat16)
    biases = normal_values(streams_of[8], (6 * D + FF,), 0.3, 1.796875, ((0, 32),))
    return dict(tokens=tokens, lengths=lengths, cotangent=cotangent, qkv_weight=qkv_weight, out_weight=out_weight, up_weight=up_weight, down_weight=down_weight, norm_gains=norm_gains, biases=biases)


EPSILON = 1e-05
NEGATIVE = -1e+30
HIGHEST = lax.Precision.HIGHEST

@jax.custom_vjp
def low(v):
    return lax.optimization_barrier(v.astype(jnp.bfloat16)).astype(jnp.float32)

@jax.custom_vjp
def low_back(v):
    return v

def low_keep(v):
    return (low(v), None)

def low_pass(kept, grad):
    return (grad,)

def back_keep(v):
    return (v, None)

def back_low(kept, grad):
    return (low(grad),)
low.defvjp(low_keep, low_pass)
low_back.defvjp(back_keep, back_low)

def layer_norm(values, gain_vec, shift_vec):
    center = values - lax.optimization_barrier(jnp.mean(values, axis=-1, keepdims=True))
    spread = lax.optimization_barrier(jnp.mean(center * center, axis=-1, keepdims=True))
    return center * lax.rsqrt(spread + EPSILON) * gain_vec + shift_vec

def gelu_tanh(values):
    return 0.5 * values * (1.0 + jnp.tanh(0.7978845608028654 * (values + 0.044715 * values * values * values)))

def block(token_rows, length_rows, qkv_flat, out_flat, up_flat, down_flat, gain_flat, bias_flat):
    count = token_rows.shape[0]
    w_qkv = qkv_flat.reshape(D, 3 * D)
    w_out = out_flat.reshape(D, D)
    w_up = up_flat.reshape(D, FF)
    w_down = down_flat.reshape(FF, D)
    gain_rows = gain_flat.reshape(2, D)
    shift_rows = bias_flat[:6 * D].reshape(6, D)
    up_bias = bias_flat[6 * D:]
    position = jnp.arange(ROWS, dtype=jnp.int32)
    first_len = length_rows[:, 0:1]
    live_end = first_len + length_rows[:, 1:2]
    segment = (position[None, :] >= first_len).astype(jnp.int32) + (position[None, :] >= live_end).astype(jnp.int32)
    allowed = (position[None, None, :] <= position[None, :, None]) & (segment[:, None, :] == segment[:, :, None])
    live_rows = (position[None, :] < live_end).astype(token_rows.dtype)
    normed = low(layer_norm(token_rows, gain_rows[0], shift_rows[0]))
    qkv_mixed = jnp.einsum('grd,de->gre', normed, w_qkv, precision=HIGHEST)
    queries = low_back(low(qkv_mixed[..., :D] + shift_rows[2])).reshape(count, ROWS, H, HD)
    key_rows = low_back(low(qkv_mixed[..., D:2 * D])).reshape(count, ROWS, H, HD)
    values = low_back(low(qkv_mixed[..., 2 * D:] + shift_rows[3])).reshape(count, ROWS, H, HD)
    scores = jnp.einsum('gqhe,gkhe->ghqk', queries, key_rows, precision=HIGHEST) * HD ** (-0.5)
    scores = low_back(scores)
    scores = jnp.where(allowed[:, None], scores, NEGATIVE)
    row_peak = lax.optimization_barrier(jnp.max(scores, axis=-1, keepdims=True))
    unnormed = jnp.exp(scores - row_peak)
    probabilities = low(unnormed / lax.optimization_barrier(jnp.sum(unnormed, axis=-1, keepdims=True)))
    context = jnp.einsum('ghqk,gkhe->gqhe', probabilities, values, precision=HIGHEST).reshape(count, ROWS, D)
    context = low_back(low(context))
    attn_out = low_back(jnp.einsum('grd,de->gre', context, w_out, precision=HIGHEST) + shift_rows[4])
    residual = token_rows + attn_out
    normed_two = low(layer_norm(residual, gain_rows[1], shift_rows[1]))
    pre_act = low_back(jnp.einsum('grd,df->grf', normed_two, w_up, precision=HIGHEST) + up_bias)
    activated = low(gelu_tanh(pre_act))
    mlp_out = jnp.einsum('grf,fd->grd', activated, w_down, precision=HIGHEST) + shift_rows[5]
    return live_rows[..., None] * (residual + mlp_out)

def reference(tokens, lengths, cotangent, qkv_weight, out_weight, up_weight, down_weight, norm_gains, biases):
    params = (qkv_weight.astype(jnp.float32), out_weight.astype(jnp.float32), up_weight.astype(jnp.float32), down_weight.astype(jnp.float32), norm_gains.astype(jnp.float32), biases.astype(jnp.float32))
    groups = BATCHES // 32
    token_all = tokens.astype(jnp.float32).reshape(groups, 32, ROWS, D)
    cot_all = cotangent.astype(jnp.float32).reshape(groups, 32, ROWS, D)
    length_all = lengths.reshape(groups, 32, 2)

    def step(carry, items):
        token_rows, length_rows, cot_rows = items

        def forward(token_rows, qkv_flat, out_flat, up_flat, down_flat, gain_flat, bias_flat):
            return block(token_rows, length_rows, qkv_flat, out_flat, up_flat, down_flat, gain_flat, bias_flat)
        result, pullback = jax.vjp(forward, token_rows, *params)
        grads = pullback(cot_rows)
        summed = tuple((older + newer for older, newer in zip(carry, grads[1:])))
        return (summed, (result, grads[0]))
    start = tuple((jnp.zeros_like(item) for item in params))
    totals, (results, grad_rows) = lax.scan(step, start, (token_all, length_all, cot_all))
    block_out = results.reshape(TOKENS, D).astype(jnp.bfloat16)
    grad_tokens = grad_rows.reshape(TOKENS, D).astype(jnp.bfloat16)
    return (block_out, grad_tokens, totals[0], totals[1], totals[2], totals[3], totals[4], totals[5])
```

```python
import functools

import jax
import jax.numpy as jnp
from jax import lax
from jax.experimental import pallas as pl
from jax.experimental.pallas import tpu as pltpu
from jax.sharding import PartitionSpec as P

D = 768
H = 12
HD = 64
FF = 3072
ROWS = 64
EPSILON = 1e-05
NEGATIVE = -1e30
MESH = pl.DeviceIdType.MESH
SHAPES = ((D, 3 * D), (D, D), (D, FF), (FF, D))
SMALL = 2 * D + 6 * D + FF
HALVES = ((0, 1, 2), (0, 2, 1))


def grid_of(devices):
    known = {32: (4, 2, 2), 256: (4, 4, 8)}
    return known.get(devices, (devices // 8, 2, 2)) + (2,)


def slab_of(rows, cols, devices):
    if rows % devices == 0 and (rows // devices) % 8 == 0:
        return rows // devices, cols
    return rows * cols // devices // 256, 256


def slabs_of(devices):
    return [slab_of(r, c, devices) for r, c in SHAPES] + [(16, 256)]


def place(dims):
    me = lax.axis_index("fsdp")
    strides = [1] * 4
    for d in (2, 1, 0):
        strides[d] = strides[d + 1] * dims[d + 1]
    at = [lax.rem(me // strides[d], dims[d]) for d in range(4)]

    def other(d, step):
        digit = lax.rem(at[d] + step, dims[d])
        return digit, me + (digit - at[d]) * strides[d]

    return at, other


def greet(dims, other):
    barrier = pltpu.get_barrier_semaphore()
    count = 0
    for d in range(4):
        for step in range(1, dims[d]):
            pl.semaphore_signal(barrier, inc=1, device_id=(other(d, step)[1],), device_id_type=MESH)
            count += 1
    pl.semaphore_wait(barrier, count)


def half_cols(ref, half):
    width = ref.shape[-1] // 2
    return pl.ds(half * width, width)


def gather_kernel(dims, n, *refs):
    ins, outs = refs[:n], refs[n : 2 * n]
    local_sem, send_sem, recv_sem = refs[2 * n :]
    at, other = place(dims)
    greet(dims, other)
    locals_ = []
    for a in range(n):
        copy = pltpu.make_async_copy(ins[a], outs[a].at[at[0], at[1], at[2], at[3]], local_sem.at[a])
        copy.start()
        locals_.append(copy)

    def send(a, half, phase):
        cols = half_cols(outs[a], half)
        order = HALVES[half]
        dim = order[phase]
        where = [slice(None) if d in order[:phase] else at[d] for d in range(4)]
        base = sum(dims[d] - 1 for d in order[:phase])
        copies = []
        for step in range(1, dims[dim]):
            target = outs[a].at[tuple(where) + (slice(None), cols)]
            source = ins[a].at[:, cols] if phase == 0 else target
            sem = (a, half, base + step - 1)
            copy = pltpu.make_async_remote_copy(
                source,
                target,
                send_sem.at[sem],
                recv_sem.at[sem],
                device_id=(other(dim, step)[1],),
                device_id_type=MESH,
            )
            copy.start()
            copies.append(copy)
        return copies

    last = sum(dims[:3]) - 3
    flying, cores = {}, {}

    def advance(a, phase):
        if phase == 1:
            locals_[a].wait()
        if phase <= 2:
            for half in range(2):
                if phase:
                    for copy in flying[a, half, phase - 1]:
                        copy.wait_recv()
                flying[a, half, phase] = send(a, half, phase)
        elif phase == 3:
            for half in range(2):
                for copy in flying[a, half, 2]:
                    copy.wait_recv()
            block = outs[a].at[:, :, :, at[3]]
            sem = (a, 0, last)
            cores[a] = pltpu.make_async_remote_copy(
                block, block, send_sem.at[sem], recv_sem.at[sem],
                device_id=(other(3, 1)[1],), device_id_type=MESH,
            )
            cores[a].start()
        else:
            cores[a].wait_recv()

    for a in range(n):
        advance(a, 0)
    for t in range(n + 3):
        for phase in range(1, 5):
            a = t - phase + 1
            if 0 <= a < n:
                advance(a, phase)
    for copies in flying.values():
        for copy in copies:
            copy.wait_send()
    for copy in cores.values():
        copy.wait_send()


def gather(parts, dims):
    n = len(parts)
    steps = sum(dims[:3]) - 2
    return pl.pallas_call(
        functools.partial(gather_kernel, dims, n),
        out_shape=[jax.ShapeDtypeStruct(dims + p.shape, p.dtype) for p in parts],
        in_specs=[pl.BlockSpec(memory_space=pl.ANY)] * n,
        out_specs=[pl.BlockSpec(memory_space=pl.ANY)] * n,
        scratch_shapes=[
            pltpu.SemaphoreType.DMA((n,)),
            pltpu.SemaphoreType.DMA((n, 2, steps)),
            pltpu.SemaphoreType.DMA((n, 2, steps)),
        ],
        compiler_params=pltpu.CompilerParams(collective_id=0, has_side_effects=True),
    )(*parts)


def add_blocks(total, terms, lead):
    count = 1
    for size in lead:
        count *= size

    def body(flat, carry):
        where, rest = [], flat
        for size in reversed(lead):
            where.insert(0, lax.rem(rest, size))
            rest = rest // size
        value = terms[0](where)[...].astype(jnp.float32)
        for term in terms[1:]:
            value = value + term(where)[...].astype(jnp.float32)
        out = total(where)
        out[...] = value.astype(out.dtype)
        return carry

    if count == 1:
        body(0, 0)
    else:
        lax.fori_loop(0, count, body, 0)


def reduce_scratch(dims, slab):
    rows, cols = slab
    shapes = [dims[:3] + slab]
    for half in range(2):
        left = [0, 1, 2]
        for dim in reversed(HALVES[half]):
            left.remove(dim)
            shapes.append((dims[dim] - 1,) + tuple(dims[d] for d in left) + (rows, cols // 2))
    return shapes


def reduce_kernel(dims, n, *refs):
    ins, outs = refs[:n], refs[n : 2 * n]
    scratch = [refs[2 * n + 7 * a : 2 * n + 7 * a + 7] for a in range(n)]
    send_sem, recv_sem = refs[9 * n :]
    at, other = place(dims)
    greet(dims, other)
    last = sum(dims[:3]) - 3
    flying = {}

    def remote(src, dst, sem, device):
        copy = pltpu.make_async_remote_copy(
            src, dst, send_sem.at[sem], recv_sem.at[sem], device_id=(device,), device_id_type=MESH
        )
        copy.start()
        return copy

    def held(a, half, phase):
        if phase == 0:
            return scratch[a][0], [0, 1, 2], half_cols(scratch[a][0], half)
        left = list(HALVES[half][: 3 - phase])
        return scratch[a][3 * half + phase].at[0], sorted(left), slice(None)

    def push(a, half, phase):
        ref, lead, cols = held(a, half, phase - 1)
        dim = HALVES[half][3 - phase]
        base = sum(dims[d] - 1 for d in HALVES[half][4 - phase :])
        copies = []
        for step in range(1, dims[dim]):
            digit, device = other(dim, step)
            where = tuple(digit if d == dim else slice(None) for d in lead)
            copies.append(
                remote(
                    ref.at[where + (slice(None), cols)],
                    scratch[a][3 * half + phase].at[step - 1],
                    (a, half, base + step - 1),
                    device,
                )
            )
        flying[a, half, phase] = copies

    def absorb(a, half, phase):
        for copy in flying[a, half, phase]:
            copy.wait_recv()
        ref, lead, cols = held(a, half, phase - 1)
        dim = HALVES[half][3 - phase]
        left = [d for d in lead if d != dim]
        landed = scratch[a][3 * half + phase]

        def own(where):
            place_of = dict(zip(left, where))
            return ref.at[tuple(at[d] if d == dim else place_of[d] for d in lead) + (slice(None), cols)]

        terms = [own] + [
            (lambda where, s=s: landed.at[(s,) + tuple(where)]) for s in range(dims[dim] - 1)
        ]
        if phase == 3:
            total = lambda where: outs[a].at[:, half_cols(outs[a], half)]
        else:
            total = lambda where: landed.at[(0,) + tuple(where)]
        add_blocks(total, terms, [dims[d] for d in left])

    def advance(a, phase):
        if phase == 0:
            flying[a, 0, 0] = [
                remote(ins[a].at[:, :, :, 1 - at[3]], scratch[a][0], (a, 0, last), other(3, 1)[1])
            ]
            return
        if phase == 1:
            for copy in flying[a, 0, 0]:
                copy.wait_recv()
            add_blocks(
                lambda w: scratch[a][0].at[tuple(w)],
                [lambda w: ins[a].at[tuple(w) + (at[3],)], lambda w: scratch[a][0].at[tuple(w)]],
                list(dims[:3]),
            )
        for half in range(2):
            if phase > 1:
                absorb(a, half, phase - 1)
            if phase < 4:
                push(a, half, phase)

    for a in range(n):
        advance(a, 0)
    for t in range(n + 3):
        for phase in range(1, 5):
            a = t - phase + 1
            if 0 <= a < n:
                advance(a, phase)
    for copies in flying.values():
        for copy in copies:
            copy.wait_send()


def reduce_scatter(parts, dims):
    n = len(parts)
    steps = sum(dims[:3]) - 2
    scratch = []
    for p in parts:
        scratch += [pltpu.VMEM(s, p.dtype) for s in reduce_scratch(dims, p.shape[4:])]
    return pl.pallas_call(
        functools.partial(reduce_kernel, dims, n),
        out_shape=[jax.ShapeDtypeStruct(p.shape[4:], jnp.float32) for p in parts],
        in_specs=[pl.BlockSpec(memory_space=pltpu.VMEM)] * n,
        out_specs=[pl.BlockSpec(memory_space=pltpu.VMEM)] * n,
        scratch_shapes=scratch
        + [
            pltpu.SemaphoreType.DMA((n, 2, steps)),
            pltpu.SemaphoreType.DMA((n, 2, steps)),
        ],
        compiler_params=pltpu.CompilerParams(
            collective_id=1, has_side_effects=True, vmem_limit_bytes=60 * 2**20
        ),
    )(*parts)


def norm_forward(values, gain, shift):
    center = values - jnp.mean(values, axis=-1, keepdims=True)
    scale = lax.rsqrt(jnp.mean(center * center, axis=-1, keepdims=True) + EPSILON)
    normal = center * scale
    return normal * gain + shift, normal, scale


def norm_backward(grad, normal, scale, gain):
    e = grad * gain
    back = scale * (
        e
        - jnp.mean(e, axis=-1, keepdims=True)
        - normal * jnp.mean(e * normal, axis=-1, keepdims=True)
    )
    return back, jnp.sum(grad * normal, axis=0), jnp.sum(grad, axis=0)


def low(values):
    return values.astype(jnp.bfloat16)


def dot(a, b, dims):
    return lax.dot_general(a, b, (dims, ((), ())), preferred_element_type=jnp.float32)


NN = ((1,), (0,))
NT = ((1,), (1,))
TN = ((0,), (0,))


def masks(lengths, rows):
    position = jnp.arange(rows, dtype=jnp.int32)
    local = position % ROWS
    batch = position // ROWS
    first = jnp.repeat(lengths[:, 0], ROWS)
    end = first + jnp.repeat(lengths[:, 1], ROWS)
    segment = (local >= first).astype(jnp.int32) + (local >= end).astype(jnp.int32) + 3 * batch
    allowed = (position[None, :] <= position[:, None]) & (segment[None, :] == segment[:, None])
    return allowed, (local < end).astype(jnp.float32)[:, None]


def block(tokens, lengths, cotangent, weights, gains, shifts, up_bias):
    w_qkv, w_out, w_up, w_down = weights
    rows = tokens.shape[0]
    scale = HD ** (-0.5)
    allowed, live = masks(lengths, rows)
    x = tokens.astype(jnp.float32)
    h1, normal1, scale1 = norm_forward(x, gains[0], shifts[0])
    h1 = low(h1)
    mixed = dot(h1, w_qkv, NN)
    q = low(mixed[:, :D] + shifts[2]).reshape(rows, H, HD).transpose(1, 0, 2)
    k = low(mixed[:, D : 2 * D]).reshape(rows, H, HD).transpose(1, 0, 2)
    v = low(mixed[:, 2 * D :] + shifts[3]).reshape(rows, H, HD).transpose(1, 0, 2)

    def bmm(spec, a, b):
        return jnp.einsum(spec, a, b, preferred_element_type=jnp.float32)

    s = jnp.where(allowed, bmm("hqe,hke->hqk", q, k) * scale, NEGATIVE)
    p = jnp.exp(s - jnp.max(s, axis=-1, keepdims=True))
    p = p / jnp.sum(p, axis=-1, keepdims=True)
    pb = low(p)
    o = low(bmm("hqk,hke->hqe", pb, v)).transpose(1, 0, 2).reshape(rows, D)
    y1 = x + dot(o, w_out, NN) + shifts[4]
    h2, normal2, scale2 = norm_forward(y1, gains[1], shifts[1])
    h2 = low(h2)
    u = dot(h2, w_up, NN) + up_bias
    t = jnp.tanh(0.7978845608028654 * (u + 0.044715 * u * u * u))
    z = low(0.5 * u * (1.0 + t))
    slope = 0.5 * (1.0 + t) + 0.5 * u * (1.0 - t * t) * 0.7978845608028654 * (
        1.0 + 3 * 0.044715 * u * u
    )
    out = low(live * (y1 + dot(z, w_down, NN) + shifts[5]))
    dy = live * cotangent.astype(jnp.float32)
    dyl = low(dy)
    du = low(dot(dyl, w_down, NT) * slope)
    g_down = low(dot(z, dyl, TN))
    dh2 = dot(du, w_up, NT)
    g_up = low(dot(h2, du, TN))
    back, gain2, shift2 = norm_backward(dh2, normal2, scale2, gains[1])
    dy1 = dy + back
    da = low(dy1)
    do = low(dot(da, w_out, NT)).reshape(rows, H, HD).transpose(1, 0, 2)
    g_out = low(dot(o, da, TN))
    dp = bmm("hqe,hke->hqk", do, v)
    dv = low(bmm("hqk,hqe->hke", pb, do))
    ds = low(p * (dp - jnp.sum(p * dp, axis=-1, keepdims=True)))
    dq = low(bmm("hqk,hke->hqe", ds, k) * scale)
    dk = low(bmm("hqk,hqe->hke", ds, q) * scale)
    dmixed = jnp.concatenate(
        [a.transpose(1, 0, 2).reshape(rows, D) for a in (dq, dk, dv)], axis=1
    )
    g_qkv = low(dot(h1, dmixed, TN))
    dh1 = dot(dmixed, w_qkv, NT)
    back, gain1, shift1 = norm_backward(dh1, normal1, scale1, gains[0])
    grad_tokens = low(dy1 + back)
    f32 = lambda a: jnp.sum(a.astype(jnp.float32), axis=0)
    sums = jnp.concatenate(
        [shift1, shift2, f32(dmixed[:, :D]), f32(dmixed[:, 2 * D :]), f32(da), f32(dyl), f32(du)]
    )
    return out, grad_tokens, (g_qkv, g_out, g_up, g_down), jnp.concatenate([gain1, gain2]), sums


def shards(dims, tokens, lengths, cotangent, w_qkv, w_out, w_up, w_down, gains, biases):
    devices = dims[0] * dims[1] * dims[2] * dims[3]
    slabs = slabs_of(devices)
    own_gain, own_bias = gains.shape[0], biases.shape[0]
    small = jnp.concatenate([gains, biases])
    small = jnp.pad(small, (0, 4096 - own_gain - own_bias))
    parts = [p.reshape(s) for p, s in zip((w_qkv, w_out, w_up, w_down, small), slabs)]
    order = (4, 0, 1, 2, 3)
    got = gather([parts[i] for i in order], dims)
    got = [got[order.index(i)] for i in range(5)]
    weights = [g.reshape(shape) for g, shape in zip(got[:4], SHAPES)]
    small = got[4].reshape(devices, 4096)
    gain_all = small[:, :own_gain].reshape(2, D).astype(jnp.float32)
    bias_all = small[:, own_gain : own_gain + own_bias].reshape(-1).astype(jnp.float32)
    out, grad_tokens, grads, gain_sums, bias_sums = block(
        tokens, lengths, cotangent, weights, gain_all, bias_all[: 6 * D].reshape(6, D), bias_all[6 * D :]
    )
    small = jnp.concatenate(
        [gain_sums.reshape(devices, own_gain), bias_sums.reshape(devices, own_bias)], axis=1
    )
    small = low(jnp.pad(small, ((0, 0), (0, 4096 - own_gain - own_bias))))
    parts = [g.reshape(dims + s) for g, s in zip(tuple(grads) + (small,), slabs)]
    order = (3, 2, 0, 1, 4)
    sums = reduce_scatter([parts[i] for i in order], dims)
    sums = [sums[order.index(i)] for i in range(5)]
    small = sums[4].reshape(-1)
    return (
        out,
        grad_tokens,
        *[g.reshape(-1) for g in sums[:4]],
        small[:own_gain],
        small[own_gain : own_gain + own_bias],
    )


def solution(mesh):
    rows, flat = P("fsdp", None), P("fsdp")
    return jax.shard_map(
        functools.partial(shards, grid_of(mesh.shape["fsdp"])),
        mesh=mesh,
        in_specs=(rows,) * 3 + (flat,) * 6,
        out_specs=(rows,) * 2 + (flat,) * 6,
        check_vma=False,
    )
```

```python
import functools

import jax
import jax.numpy as jnp
from jax import lax
from jax.experimental import pallas as pl
from jax.experimental.pallas import tpu as pltpu
from jax.sharding import PartitionSpec as P

D = 768
H = 12
HD = 64
FF = 3072
ROWS = 64
EPSILON = 1e-05
NEGATIVE = -1e30
MESH = pl.DeviceIdType.MESH
SHAPES = ((D, 3 * D), (D, D), (D, FF), (FF, D))
LAG = 1
HALVES = ((0, 1, 2), (0, 2, 1))


def grid_of(devices):
    known = {32: (4, 2, 2), 256: (4, 4, 8)}
    return known.get(devices, (devices // 8, 2, 2)) + (2,)


def slab_of(rows, cols, devices):
    if rows % devices == 0 and (rows // devices) % 8 == 0:
        return rows // devices, cols
    return rows * cols // devices // 256, 256


def slabs_of(devices):
    return [slab_of(r, c, devices) for r, c in SHAPES] + [(16, 256)]


def place(dims):
    me = lax.axis_index("fsdp")
    strides = [1] * 4
    for d in (2, 1, 0):
        strides[d] = strides[d + 1] * dims[d + 1]
    at = [lax.rem(me // strides[d], dims[d]) for d in range(4)]

    def other(d, step):
        digit = lax.rem(at[d] + step, dims[d])
        return digit, me + (digit - at[d]) * strides[d]

    return at, other


def greet(dims, other):
    barrier = pltpu.get_barrier_semaphore()
    count = 0
    for d in range(4):
        for step in range(1, dims[d]):
            pl.semaphore_signal(barrier, inc=1, device_id=(other(d, step)[1],), device_id_type=MESH)
            count += 1
    pl.semaphore_wait(barrier, count)


def chunks_of(slabs, order):
    chunks = []
    for a in order:
        rows, cols = slabs[a]
        if rows >= 96 and rows % 32 == 0:
            chunks += [(a, r, rows // 2, 0, cols) for r in (0, rows // 2)]
        elif cols > 768 and cols % 768 == 0:
            chunks += [(a, 0, rows, i * (cols // 3), cols // 3) for i in range(3)]
        else:
            chunks.append((a, 0, rows, 0, cols))
    return chunks


def window(chunk, half=None):
    a, row, rows, col, cols = chunk
    if half is None:
        return pl.ds(row, rows), pl.ds(col, cols)
    return pl.ds(row, rows), pl.ds(col + half * (cols // 2), cols // 2)


def gather_kernel(dims, n, chunks, *refs):
    ins, outs = refs[:n], refs[n : 2 * n]
    local_sem, send_sem, recv_sem = refs[2 * n :]
    at, other = place(dims)
    greet(dims, other)
    locals_ = []
    for a in range(n):
        copy = pltpu.make_async_copy(ins[a], outs[a].at[at[0], at[1], at[2], at[3]], local_sem.at[a])
        copy.start()
        locals_.append(copy)

    waited = set()

    def send(i, half, phase):
        a = chunks[i][0]
        view = window(chunks[i], half)
        order = HALVES[half]
        dim = order[phase]
        where = [slice(None) if d in order[:phase] else at[d] for d in range(4)]
        base = sum(dims[d] - 1 for d in order[:phase])
        copies = []
        for step in range(1, dims[dim]):
            target = outs[a].at[tuple(where) + view]
            source = ins[a].at[view] if phase == 0 else target
            sem = (i, half, base + step - 1)
            copy = pltpu.make_async_remote_copy(
                source,
                target,
                send_sem.at[sem],
                recv_sem.at[sem],
                device_id=(other(dim, step)[1],),
                device_id_type=MESH,
            )
            copy.start()
            copies.append(copy)
        return copies

    last = sum(dims[:3]) - 3
    flying, cores = {}, {}

    def advance(i, phase):
        a = chunks[i][0]
        if phase == 1 and a not in waited:
            waited.add(a)
            locals_[a].wait()
        if phase <= 2:
            for half in range(2):
                if phase:
                    for copy in flying[i, half, phase - 1]:
                        copy.wait_recv()
                flying[i, half, phase] = send(i, half, phase)
        elif phase == 3:
            for half in range(2):
                for copy in flying[i, half, 2]:
                    copy.wait_recv()
            block = outs[a].at[(slice(None),) * 3 + (at[3],) + window(chunks[i])]
            sem = (i, 0, last)
            cores[i] = pltpu.make_async_remote_copy(
                block,
                block,
                send_sem.at[sem],
                recv_sem.at[sem],
                device_id=(other(3, 1)[1],),
                device_id_type=MESH,
            )
            cores[i].start()
        else:
            cores[i].wait_recv()

    count = len(chunks)
    for i in range(count):
        advance(i, 0)
    for t in range(count + 3):
        for phase in range(1, 5):
            i = t - phase + 1
            if 0 <= i < count:
                advance(i, phase)
    for copies in flying.values():
        for copy in copies:
            copy.wait_send()
    for copy in cores.values():
        copy.wait_send()


def gather(parts, dims, order):
    n = len(parts)
    chunks = chunks_of([p.shape for p in parts], order)
    steps = sum(dims[:3]) - 2
    return pl.pallas_call(
        functools.partial(gather_kernel, dims, n, chunks),
        out_shape=[jax.ShapeDtypeStruct(dims + p.shape, p.dtype) for p in parts],
        in_specs=[pl.BlockSpec(memory_space=pl.ANY)] * n,
        out_specs=[pl.BlockSpec(memory_space=pl.ANY)] * n,
        scratch_shapes=[
            pltpu.SemaphoreType.DMA((n,)),
            pltpu.SemaphoreType.DMA((len(chunks), 2, steps)),
            pltpu.SemaphoreType.DMA((len(chunks), 2, steps)),
        ],
        compiler_params=pltpu.CompilerParams(collective_id=0, has_side_effects=True),
    )(*parts)


def add_blocks(total, terms, lead):
    count = 1
    for size in lead:
        count *= size

    def body(flat, carry):
        where, rest = [], flat
        for size in reversed(lead):
            where.insert(0, lax.rem(rest, size))
            rest = rest // size
        value = terms[0](where)[...].astype(jnp.float32)
        for term in terms[1:]:
            value = value + term(where)[...].astype(jnp.float32)
        out = total(where)
        out[...] = value.astype(out.dtype)
        return carry

    if count == 1:
        body(0, 0)
    else:
        lax.fori_loop(0, count, body, 0)


def reduce_scratch(dims, slab):
    rows, cols = slab
    shapes = [dims[:3] + slab]
    for half in range(2):
        left = [0, 1, 2]
        for dim in reversed(HALVES[half]):
            left.remove(dim)
            shapes.append((dims[dim] - 1,) + tuple(dims[d] for d in left) + (rows, cols // 2))
    return shapes


def weight_gradient(left, right, turned, part):
    rows, (slab_rows, cols) = left.shape[1], part.shape[4:]
    step = 512 if rows <= D and cols % 512 == 0 else 256
    flipped = turned.at[pl.ds(0, rows)]
    flipped[...] = left[...].T
    depth = min(rows, D)
    lead = part.shape[0] * depth // rows

    def body(j, carry):
        view = pl.ds(pl.multiple_of(j * step, step), step)
        for i in range(rows // depth):
            value = jnp.dot(
                turned[pl.ds(i * depth, depth)], right[:, view], preferred_element_type=jnp.float32
            )
            value = value.reshape((lead,) + part.shape[1:4] + (slab_rows, step))
            part[pl.ds(i * lead, lead), :, :, :, :, view] = value.astype(part.dtype)
        return carry

    lax.fori_loop(0, cols // step, body, 0)


def reduce_kernel(dims, n, chunks, fused, *refs):
    count = len(chunks)
    if fused:
        pairs, given, refs = refs[: 2 * n - 2], refs[2 * n - 2], refs[2 * n - 1 :]
        outs, parts, turned, refs = refs[:n], refs[n : 2 * n - 1], refs[2 * n - 1], refs[2 * n :]
        ins = list(parts) + [given]
    else:
        ins, outs, refs = refs[:n], refs[n : 2 * n], refs[2 * n :]
    scratch = [refs[7 * i : 7 * i + 7] for i in range(count)]
    send_sem, recv_sem = refs[7 * count :]
    at, other = place(dims)
    greet(dims, other)
    last = sum(dims[:3]) - 3
    flying = {}

    def remote(src, dst, sem, device):
        copy = pltpu.make_async_remote_copy(
            src, dst, send_sem.at[sem], recv_sem.at[sem], device_id=(device,), device_id_type=MESH
        )
        copy.start()
        return copy

    def held(a, half, phase):
        if phase == 0:
            width = chunks[a][4] // 2
            return scratch[a][0], [0, 1, 2], pl.ds(half * width, width)
        left = list(HALVES[half][: 3 - phase])
        return scratch[a][3 * half + phase].at[0], sorted(left), slice(None)

    def push(a, half, phase):
        ref, lead, cols = held(a, half, phase - 1)
        dim = HALVES[half][3 - phase]
        base = sum(dims[d] - 1 for d in HALVES[half][4 - phase :])
        copies = []
        for step in range(1, dims[dim]):
            digit, device = other(dim, step)
            where = tuple(digit if d == dim else slice(None) for d in lead)
            copies.append(
                remote(
                    ref.at[where + (slice(None), cols)],
                    scratch[a][3 * half + phase].at[step - 1],
                    (a, half, base + step - 1),
                    device,
                )
            )
        flying[a, half, phase] = copies

    def absorb(a, half, phase):
        for copy in flying[a, half, phase]:
            copy.wait_recv()
        ref, lead, cols = held(a, half, phase - 1)
        dim = HALVES[half][3 - phase]
        left = [d for d in lead if d != dim]
        landed = scratch[a][3 * half + phase]

        def own(where):
            place_of = dict(zip(left, where))
            return ref.at[tuple(at[d] if d == dim else place_of[d] for d in lead) + (slice(None), cols)]

        terms = [own] + [
            (lambda where, s=s: landed.at[(s,) + tuple(where)]) for s in range(dims[dim] - 1)
        ]
        if phase == 3:
            total = lambda where: outs[chunks[a][0]].at[window(chunks[a], half)]
        else:
            total = lambda where: landed.at[(0,) + tuple(where)]
        add_blocks(total, terms, [dims[d] for d in left])

    def advance(a, phase):
        if phase == 0:
            flying[a, 0, 0] = [
                remote(
                    ins[chunks[a][0]].at[(slice(None),) * 3 + (1 - at[3],) + window(chunks[a])],
                    scratch[a][0],
                    (a, 0, last),
                    other(3, 1)[1],
                )
            ]
            return
        if phase == 1:
            for copy in flying[a, 0, 0]:
                copy.wait_recv()
            add_blocks(
                lambda w: scratch[a][0].at[tuple(w)],
                [
                    lambda w: ins[chunks[a][0]].at[tuple(w) + (at[3],) + window(chunks[a])],
                    lambda w: scratch[a][0].at[tuple(w)],
                ],
                list(dims[:3]),
            )
        for half in range(2):
            if phase > 1:
                absorb(a, half, phase - 1)
            if phase < 4:
                push(a, half, phase)

    made = set()
    for t in range(count + LAG + 4):
        if t < count:
            array = chunks[t][0]
            if fused and array not in made and array < n - 1:
                weight_gradient(pairs[2 * array], pairs[2 * array + 1], turned, ins[array])
            made.add(array)
            advance(t, 0)
        for phase in range(1, 5):
            a = t - phase + 1 - LAG
            if 0 <= a < count:
                advance(a, phase)
    for copies in flying.values():
        for copy in copies:
            copy.wait_send()


def reduce_scatter(parts, pairs, dims, slabs, order):
    n = len(slabs)
    steps = sum(dims[:3]) - 2
    chunks = chunks_of(slabs, order)
    scratch = []
    if pairs:
        scratch += [pltpu.VMEM(dims + s, jnp.bfloat16) for s in slabs[:-1]]
        scratch.append(pltpu.VMEM((FF, pairs[0].shape[0]), jnp.bfloat16))
    for chunk in chunks:
        shapes = reduce_scratch(dims, (chunk[2], chunk[4]))
        scratch += [pltpu.VMEM(s, jnp.bfloat16) for s in shapes]
    operands = list(pairs) + list(parts)
    return pl.pallas_call(
        functools.partial(reduce_kernel, dims, n, chunks, bool(pairs)),
        out_shape=[jax.ShapeDtypeStruct(s, jnp.float32) for s in slabs],
        in_specs=[pl.BlockSpec(memory_space=pltpu.VMEM)] * len(operands),
        out_specs=[pl.BlockSpec(memory_space=pltpu.VMEM)] * n,
        scratch_shapes=scratch
        + [
            pltpu.SemaphoreType.DMA((len(chunks), 2, steps)),
            pltpu.SemaphoreType.DMA((len(chunks), 2, steps)),
        ],
        compiler_params=pltpu.CompilerParams(
            collective_id=1, has_side_effects=True, vmem_limit_bytes=62 * 2**20
        ),
    )(*operands)


def norm_forward(values, gain, shift):
    center = values - jnp.mean(values, axis=-1, keepdims=True)
    scale = lax.rsqrt(jnp.mean(center * center, axis=-1, keepdims=True) + EPSILON)
    normal = center * scale
    return normal * gain + shift, normal, scale


def norm_backward(grad, normal, scale, gain):
    e = grad * gain
    back = scale * (
        e
        - jnp.mean(e, axis=-1, keepdims=True)
        - normal * jnp.mean(e * normal, axis=-1, keepdims=True)
    )
    return back, jnp.sum(grad * normal, axis=0), jnp.sum(grad, axis=0)


def low(values):
    return values.astype(jnp.bfloat16)


def dot(a, b, dims):
    return lax.dot_general(a, b, (dims, ((), ())), preferred_element_type=jnp.float32)


NN = ((1,), (0,))
NT = ((1,), (1,))
TN = ((0,), (0,))


def masks(lengths, rows):
    position = jnp.arange(rows, dtype=jnp.int32)
    local = position % ROWS
    batch = position // ROWS
    first = jnp.repeat(lengths[:, 0], ROWS)
    end = first + jnp.repeat(lengths[:, 1], ROWS)
    segment = (local >= first).astype(jnp.int32) + (local >= end).astype(jnp.int32) + 3 * batch
    allowed = (position[None, :] <= position[:, None]) & (segment[None, :] == segment[:, None])
    return allowed, (local < end).astype(jnp.float32)[:, None]


def block(tokens, lengths, cotangent, weights, gains, shifts, up_bias):
    w_qkv, w_out, w_up, w_down = weights
    rows = tokens.shape[0]
    scale = HD ** (-0.5)
    allowed, live = masks(lengths, rows)
    x = tokens.astype(jnp.float32)
    h1, normal1, scale1 = norm_forward(x, gains[0], shifts[0])
    h1 = low(h1)
    mixed = dot(h1, w_qkv, NN)
    q = low(mixed[:, :D] + shifts[2]).reshape(rows, H, HD).transpose(1, 0, 2)
    k = low(mixed[:, D : 2 * D]).reshape(rows, H, HD).transpose(1, 0, 2)
    v = low(mixed[:, 2 * D :] + shifts[3]).reshape(rows, H, HD).transpose(1, 0, 2)

    def bmm(spec, a, b):
        return jnp.einsum(spec, a, b, preferred_element_type=jnp.float32)

    s = jnp.where(allowed, bmm("hqe,hke->hqk", q, k) * scale, NEGATIVE)
    p = jnp.exp(s - jnp.max(s, axis=-1, keepdims=True))
    p = p / jnp.sum(p, axis=-1, keepdims=True)
    pb = low(p)
    o = low(bmm("hqk,hke->hqe", pb, v)).transpose(1, 0, 2).reshape(rows, D)
    y1 = x + dot(o, w_out, NN) + shifts[4]
    h2, normal2, scale2 = norm_forward(y1, gains[1], shifts[1])
    h2 = low(h2)
    u = dot(h2, w_up, NN) + up_bias
    t = jnp.tanh(0.7978845608028654 * (u + 0.044715 * u * u * u))
    z = low(0.5 * u * (1.0 + t))
    slope = 0.5 * (1.0 + t) + 0.5 * u * (1.0 - t * t) * 0.7978845608028654 * (
        1.0 + 3 * 0.044715 * u * u
    )
    out = low(live * (y1 + dot(z, w_down, NN) + shifts[5]))
    dy = live * cotangent.astype(jnp.float32)
    dyl = low(dy)
    du = low(dot(dyl, w_down, NT) * slope)
    dh2 = dot(du, w_up, NT)
    back, gain2, shift2 = norm_backward(dh2, normal2, scale2, gains[1])
    dy1 = dy + back
    da = low(dy1)
    do = low(dot(da, w_out, NT)).reshape(rows, H, HD).transpose(1, 0, 2)
    dp = bmm("hqe,hke->hqk", do, v)
    dv = low(bmm("hqk,hqe->hke", pb, do))
    ds = low(p * (dp - jnp.sum(p * dp, axis=-1, keepdims=True)))
    dq = low(bmm("hqk,hke->hqe", ds, k) * scale)
    dk = low(bmm("hqk,hqe->hke", ds, q) * scale)
    dmixed = jnp.concatenate(
        [a.transpose(1, 0, 2).reshape(rows, D) for a in (dq, dk, dv)], axis=1
    )
    dh1 = dot(dmixed, w_qkv, NT)
    back, gain1, shift1 = norm_backward(dh1, normal1, scale1, gains[0])
    grad_tokens = low(dy1 + back)
    f32 = lambda a: jnp.sum(a.astype(jnp.float32), axis=0)
    sums = jnp.concatenate(
        [shift1, shift2, f32(dmixed[:, :D]), f32(dmixed[:, 2 * D :]), f32(da), f32(dyl), f32(du)]
    )
    pairs = (h1, dmixed, o, da, h2, du, z, dyl)
    return out, grad_tokens, pairs, jnp.concatenate([gain1, gain2]), sums


def shards(dims, tokens, lengths, cotangent, w_qkv, w_out, w_up, w_down, gains, biases):
    devices = dims[0] * dims[1] * dims[2] * dims[3]
    slabs = slabs_of(devices)
    own_gain, own_bias = gains.shape[0], biases.shape[0]
    small = jnp.concatenate([gains, biases])
    small = jnp.pad(small, (0, 4096 - own_gain - own_bias))
    parts = [p.reshape(s) for p, s in zip((w_qkv, w_out, w_up, w_down, small), slabs)]
    got = gather(parts, dims, (4, 1, 0, 2, 3))
    weights = [g.reshape(shape) for g, shape in zip(got[:4], SHAPES)]
    small = got[4].reshape(devices, 4096)
    gain_all = small[:, :own_gain].reshape(2, D).astype(jnp.float32)
    bias_all = small[:, own_gain : own_gain + own_bias].reshape(-1).astype(jnp.float32)
    out, grad_tokens, pairs, gain_sums, bias_sums = block(
        tokens, lengths, cotangent, weights, gain_all, bias_all[: 6 * D].reshape(6, D), bias_all[6 * D :]
    )
    small = jnp.concatenate(
        [gain_sums.reshape(devices, own_gain), bias_sums.reshape(devices, own_bias)], axis=1
    )
    small = low(jnp.pad(small, ((0, 0), (0, 4096 - own_gain - own_bias))))
    small = small.reshape(dims + slabs[4])
    order = (3, 2, 0, 1, 4)
    if all(slab[1] == shape[1] for slab, shape in zip(slabs, SHAPES)):
        sums = reduce_scatter([small], pairs, dims, slabs, order)
    else:
        grads = [low(dot(pairs[2 * i], pairs[2 * i + 1], TN)) for i in range(4)]
        parts = [g.reshape(dims + s) for g, s in zip(grads, slabs)]
        sums = reduce_scatter(parts + [small], (), dims, slabs, order)
    small = sums[4].reshape(-1)
    return (
        out,
        grad_tokens,
        *[g.reshape(-1) for g in sums[:4]],
        small[:own_gain],
        small[own_gain : own_gain + own_bias],
    )


def solution(mesh):
    rows, flat = P("fsdp", None), P("fsdp")
    return jax.shard_map(
        functools.partial(shards, grid_of(mesh.shape["fsdp"])),
        mesh=mesh,
        in_specs=(rows,) * 3 + (flat,) * 6,
        out_specs=(rows,) * 2 + (flat,) * 6,
        check_vma=False,
    )
```
